128 devices in a mesh: fsdp: 16 (over z, y_lo, core), tp: 8 (over y_hi, x).
Axes of the slice: x: 4, y: 4 (y_hi: 2, y_lo: 2; y = y_hi * 2 + y_lo), z: 4, core: 2. Of those that a mesh axis runs over, the one named last changes fastest.
Arguments:
- tokens: bfloat16 [2, 2304, 8192], P(None, 'fsdp'), may hold values from -6 to 6
- w_query: bfloat16 [8192, 8192], P('fsdp', 'tp'), may hold values from -0.0625 to 0.0625
- w_keyval: bfloat16 [8192, 2, 1024], P('fsdp', None, 'tp'), may hold values from -0.0625 to 0.0625
- b_query: bfloat16 [8192], P('tp')
- b_keyval: bfloat16 [2, 1024], P(None, 'tp'), may hold values from -3 to 3
- rotary_perm: int32 [128], replicated, may hold values from 0 to 127, each once
- cache: bfloat16 [2, 2304, 8, 256, 128], P(None, 'fsdp', 'tp')
- lengths: int32 [2304], P('fsdp'), may hold values from 2 to 256
Outputs:
- attention: bfloat16 [2, 2304, 8192], P(None, 'fsdp', 'tp')
The draws below stay inside these ranges and needn't reach their ends.
All inputs are finite; a program needn't handle non-finite values.
Results may differ from the reference program's by a relative error of at most 0.0063.
Values may be sent and summed in bfloat16 or wider, within the bound.
No kernel may reach another device: no remote copies, remote signals or barrier semaphores. Data moves between devices by JAX's collectives and lax.ppermute only.
A program may use at most 128 MiB of HBM per device.

```python
import jax
import jax.numpy as jnp
from jax import lax

D = 8192
HQ = 64
HK = 8
HD = 128
STEPS = 2
CACHE = 256
ROWS_ALL = 2304
N_TP = 8


def draw_b_query(key, part):
    key = jax.random.fold_in(key, 11)
    noise = jax.random.normal(key, (HQ * HD,), jnp.float32)
    return (0.5 * noise).astype(jnp.bfloat16)


def draw_cache(key, part):
    key = jax.random.fold_in(key, 23)
    values = jax.random.normal(key, (2, ROWS_ALL, HK, CACHE, HD), jnp.float32)
    return values.astype(jnp.bfloat16)


def touch_ends(array, rng, low, top_value):
    place = [jax.random.randint(jax.random.fold_in(rng, axis), (), 0, length) for axis, length in enumerate(array.shape)]
    widest = array.shape.index(max(array.shape))
    beside = place[:widest] + [(place[widest] + 1) % array.shape[widest]] + place[widest + 1:]
    return array.at[tuple(place)].set(low).at[tuple(beside)].set(top_value)


def block_levels(rng, extent, pieces, least, largest):
    level, own = 1.0, jax.random.fold_in(rng, 6)
    for axis_at, shards_of in pieces:
        heights = jnp.exp(jax.random.uniform(jax.random.fold_in(own, axis_at), (shards_of,), jnp.float32, least / len(pieces), largest / len(pieces)))
        level = level * jnp.repeat(heights, extent[axis_at] // shards_of).reshape([-1 if axis == axis_at else 1 for axis in range(len(extent))])
    return level


def centred(stream_key, dims, spread, limit, cuts=(), kind=jnp.bfloat16):
    entries = spread * jax.random.normal(stream_key, dims, jnp.float32)
    if cuts:
        entries = entries * block_levels(stream_key, dims, cuts, -0.22, 0.18)
    return jnp.clip(entries, -limit, limit).astype(kind)


def setup_inputs(seed: int = 0) -> dict:
    seeds = jax.random.split(jax.random.key(seed), 9)
    return {
        "tokens": centred(seeds[0], (STEPS, ROWS_ALL, D), 1.0, 6.0, ((1, 16),)),
        "w_query": centred(seeds[1], (D, HQ * HD), D ** -0.5, 0.0625, ((0, 16), (1, 8))),
        "w_keyval": centred(seeds[2], (D, 2, HK * HD), D ** -0.5, 0.0625, ((0, 16), (2, 8))),
        "b_query": draw_b_query(jax.random.fold_in(seeds[8], 71), 0),
        "b_keyval": centred(seeds[4], (2, HK * HD), 0.5, 3.0, ((1, 8),)),
        "rotary_perm": jax.random.permutation(seeds[5], HD).astype(jnp.int32),
        "cache": draw_cache(jax.random.fold_in(seeds[8], 71), 0),
        "lengths": touch_ends(jax.random.randint(seeds[7], (ROWS_ALL,), 2, CACHE + 1), jax.random.fold_in(seeds[7], 1), 2, CACHE).astype(jnp.int32),
    }


rope_base = 1000000.0
neg_large = -1.0e30


def rotate(vectors, position):
    head_size = vectors.shape[-1]
    half_size = head_size // 2
    pair_index = jnp.arange(half_size, dtype=jnp.float32)
    inverse = rope_base ** (-2.0 * pair_index / head_size)
    angles = position * inverse
    cos_part = jnp.cos(angles)
    sin_part = jnp.sin(angles)
    first_half = vectors[..., :half_size]
    second = vectors[..., half_size:]
    return jnp.concatenate([first_half * cos_part - second * sin_part, second * cos_part + first_half * sin_part], axis=-1)


def attend(queries, key_new, value_new, cache, lengths):
    score_scale = queries.shape[-1] ** -0.5
    query_wide = queries.astype(jnp.float32)
    cached_scores = jnp.einsum('srgqd,rgcd->srgqc', query_wide, cache[0].astype(jnp.float32)) * score_scale
    fresh_scores = jnp.einsum('srgqd,trgd->srgqt', query_wide, key_new.astype(jnp.float32)) * score_scale
    slots = jnp.arange(cache.shape[3], dtype=jnp.int32)
    visible_old = (slots[None, :] < lengths[:, None])[None, :, None, None, :]
    step_ids = jnp.arange(queries.shape[0], dtype=jnp.int32)
    visible_new = (step_ids[None, :] <= step_ids[:, None])[:, None, None, None, :]
    cached_scores = jnp.where(visible_old, cached_scores, neg_large)
    fresh_scores = jnp.where(visible_new, fresh_scores, neg_large)
    row_max = jnp.maximum(jnp.max(cached_scores, axis=-1), jnp.max(fresh_scores, axis=-1))[..., None]
    cached_exp = jnp.exp(cached_scores - row_max)
    fresh_exp = jnp.exp(fresh_scores - row_max)
    denominator = jnp.sum(cached_exp, axis=-1, keepdims=True) + jnp.sum(fresh_exp, axis=-1, keepdims=True)
    cached_weights = (cached_exp / denominator).astype(jnp.bfloat16)
    fresh_weights = (fresh_exp / denominator).astype(jnp.bfloat16)
    result = jnp.einsum('srgqc,rgcd->srgqd', cached_weights.astype(jnp.float32), cache[1].astype(jnp.float32))
    result = result + jnp.einsum('srgqt,trgd->srgqd', fresh_weights.astype(jnp.float32), value_new.astype(jnp.float32))
    return result.astype(jnp.bfloat16)


def reference(tokens, w_query, w_keyval, b_query, b_keyval, rotary_perm, cache, lengths):
    step_count, row_count, model_width = tokens.shape
    per_group = HQ // HK
    per_shard = HK // N_TP
    slot_ids = jnp.arange(HK, dtype=jnp.int32)
    head_order = (((slot_ids // per_shard) + N_TP // 2) % N_TP) * per_shard + (per_shard - 1 - slot_ids % per_shard)
    flattened = tokens.reshape(step_count * row_count, model_width)
    queries = jnp.dot(flattened, w_query, preferred_element_type=jnp.float32) + b_query.astype(jnp.float32)
    key_part = jnp.dot(flattened, w_keyval[:, 0, :], preferred_element_type=jnp.float32) + b_keyval[0].astype(jnp.float32)
    value_part = jnp.dot(flattened, w_keyval[:, 1, :], preferred_element_type=jnp.float32) + b_keyval[1].astype(jnp.float32)
    queries = queries.astype(jnp.bfloat16).reshape(step_count, row_count, HK, per_group, HD)
    key_part = key_part.astype(jnp.bfloat16).reshape(step_count, row_count, HK, HD)
    value_part = value_part.astype(jnp.bfloat16).reshape(step_count, row_count, HK, HD)
    queries = jnp.take(jnp.take(queries, head_order, axis=2), rotary_perm, axis=4)
    key_part = jnp.take(jnp.take(key_part, head_order, axis=2), rotary_perm, axis=3)
    value_part = jnp.take(value_part, head_order, axis=2)
    positions = (lengths[None, :] + jnp.arange(step_count, dtype=jnp.int32)[:, None]).astype(jnp.float32)
    query_rot = rotate(queries.astype(jnp.float32), positions[:, :, None, None, None]).astype(jnp.bfloat16)
    key_rot = rotate(key_part.astype(jnp.float32), positions[:, :, None, None]).astype(jnp.bfloat16)

    def one_group(group_id):
        return attend(lax.dynamic_slice_in_dim(query_rot, group_id, 1, 2),
                      lax.dynamic_slice_in_dim(key_rot, group_id, 1, 2),
                      lax.dynamic_slice_in_dim(value_part, group_id, 1, 2),
                      lax.dynamic_slice_in_dim(cache, group_id, 1, 2), lengths)

    per_group_out = lax.map(one_group, jnp.arange(HK, dtype=jnp.int32))
    stacked = jnp.moveaxis(per_group_out[:, :, :, 0], 0, 2)
    return stacked.reshape(step_count, row_count, HQ * HD)
```

```python
import jax
import jax.numpy as jnp
from jax import lax
from jax.sharding import PartitionSpec as P

HQ = 64
HK = 8
HD = 128

rope_base = 1000000.0
neg_large = -1e30

AXES = ("fsdp", "tp")
N_Z = 4
N_TP = 8


def place_of(index):
    f, t = divmod(index, N_TP)
    z, rest = divmod(f, 4)
    y_lo, core = divmod(rest, 2)
    y_hi, x = divmod(t, 4)
    return z, y_hi * 2 + y_lo, x, core


def index_of(z, y, x, core):
    z, y, x, core = z % 4, y % 4, x % 4, core % 2
    return (z * 4 + (y % 2) * 2 + core) * N_TP + (y // 2) * 4 + x


def moved(value, to):
    pairs = [(i, index_of(*to(*place_of(i)))) for i in range(128)]
    return lax.ppermute(value, AXES, pairs)


def z_by(step):
    return lambda z, y, x, core: (z + step, y, x, core)


def other_core(z, y, x, core):
    return z, y, x, 1 - core


def inner_y(z, y, x, core):
    return z, y ^ 1, x, core


def cross_y_core(z, y, x, core):
    return z, 3 - y, x, 1 - core


def cross_y(z, y, x, core):
    return z, 3 - y, x, core


def far_y(z, y, x, core):
    return z, y + 2, x, core


def rotate(vectors, position):
    head_size = vectors.shape[-1]
    half_size = head_size // 2
    pair_index = jnp.arange(half_size, dtype=jnp.float32)
    inverse = rope_base ** (-2.0 * pair_index / head_size)
    angles = position * inverse
    cos_part = jnp.cos(angles)
    sin_part = jnp.sin(angles)
    first_half = vectors[..., :half_size]
    second = vectors[..., half_size:]
    return jnp.concatenate(
        [first_half * cos_part - second * sin_part, second * cos_part + first_half * sin_part],
        axis=-1,
    )


def attend(queries, key_new, value_new, cache, lengths):
    score_scale = queries.shape[-1] ** (-0.5)
    cached_scores = (
        jnp.einsum("srgqd,rgcd->srgqc", queries, cache[0], preferred_element_type=jnp.float32)
        * score_scale
    )
    fresh_scores = (
        jnp.einsum("srgqd,trgd->srgqt", queries, key_new, preferred_element_type=jnp.float32)
        * score_scale
    )
    slots = jnp.arange(cache.shape[3], dtype=jnp.int32)
    visible_old = (slots[None, :] < lengths[:, None])[None, :, None, None, :]
    step_ids = jnp.arange(queries.shape[0], dtype=jnp.int32)
    visible_new = (step_ids[None, :] <= step_ids[:, None])[:, None, None, None, :]
    cached_scores = jnp.where(visible_old, cached_scores, neg_large)
    fresh_scores = jnp.where(visible_new, fresh_scores, neg_large)
    row_max = jnp.maximum(jnp.max(cached_scores, axis=-1), jnp.max(fresh_scores, axis=-1))[
        ..., None
    ]
    cached_exp = jnp.exp(cached_scores - row_max)
    fresh_exp = jnp.exp(fresh_scores - row_max)
    denominator = jnp.sum(cached_exp, axis=-1, keepdims=True) + jnp.sum(
        fresh_exp, axis=-1, keepdims=True
    )
    cached_weights = (cached_exp / denominator).astype(jnp.bfloat16)
    fresh_weights = (fresh_exp / denominator).astype(jnp.bfloat16)
    result = jnp.einsum(
        "srgqc,rgcd->srgqd", cached_weights, cache[1], preferred_element_type=jnp.float32
    )
    result = result + jnp.einsum(
        "srgqt,trgd->srgqd", fresh_weights, value_new, preferred_element_type=jnp.float32
    )
    return result.astype(jnp.bfloat16)


def gathered_over_z(block):
    return [block, moved(block, z_by(1)), moved(block, z_by(-1)), moved(block, z_by(2))]


def row_sets(tokens):
    f = lax.axis_index("fsdp")
    z, y_lo, core = f // 4, (f // 2) % 2, f % 2
    flat = tokens.reshape(-1, tokens.shape[-1])
    share = flat.shape[1] // 16

    def slab(dy, dc):
        parts = []
        for dz in (0, -1, 1, 2):
            block = ((z + dz) % 4) * 4 + (y_lo ^ dy) * 2 + (core ^ dc)
            parts.append(lax.dynamic_slice_in_dim(flat, block * share, share, 1))
        return jnp.concatenate(parts, axis=1)

    return {
        (0, 0): slab(0, 0),
        (0, 1): moved(slab(0, 1), other_core),
        (1, 0): moved(slab(1, 0), inner_y),
        (1, 1): moved(slab(1, 1), cross_y_core),
    }


def returned(rows, blocks, bias):
    weights = jnp.concatenate(blocks, axis=0)
    sums = {
        key: jnp.dot(value, weights, preferred_element_type=jnp.float32)
        for key, value in rows.items()
    }
    partner = moved(
        jnp.stack([sums[0, 1].astype(jnp.bfloat16), sums[1, 1].astype(jnp.bfloat16)]), other_core
    ).astype(jnp.float32)
    same = sums[0, 0] + partner[0] + bias.astype(jnp.float32)
    other = sums[1, 0] + partner[1]
    same = moved(same.astype(jnp.bfloat16), far_y)
    other = moved(other.astype(jnp.bfloat16), cross_y)
    return (same.astype(jnp.float32) + other.astype(jnp.float32)).astype(jnp.bfloat16)


def body(tokens, w_query, w_keyval, b_query, b_keyval, rotary_perm, cache, lengths):
    step_count, row_count, model_width = tokens.shape
    per_group = HQ // HK
    head_size = rotary_perm.shape[0]

    early = 3 * head_size
    first = jnp.concatenate([w_keyval[:, 0], w_keyval[:, 1], w_query[:, :early]], axis=1)
    second = w_query[:, early:]
    first_bias = jnp.concatenate([b_keyval[0], b_keyval[1], b_query[:early]])
    rows = row_sets(tokens)
    first_blocks = gathered_over_z(first)
    second, first_blocks = lax.optimization_barrier((second, first_blocks))
    second_blocks = gathered_over_z(second)
    first_sums = returned(rows, first_blocks, first_bias)
    second_sums = returned(rows, second_blocks, b_query[early:])

    queries = jnp.concatenate([first_sums[:, 2 * head_size :], second_sums], axis=1)
    queries = queries.reshape(step_count, row_count, 1, per_group, head_size)
    queries = jnp.take(queries, rotary_perm, axis=4)
    key_part = first_sums[:, :head_size].reshape(step_count, row_count, 1, head_size)
    key_part = jnp.take(key_part, rotary_perm, axis=3)
    value_part = first_sums[:, head_size : 2 * head_size]
    value_part = value_part.reshape(step_count, row_count, 1, head_size)
    positions = (lengths[None, :] + jnp.arange(step_count, dtype=jnp.int32)[:, None]).astype(
        jnp.float32
    )
    query_rot = rotate(queries.astype(jnp.float32), positions[:, :, None, None, None]).astype(
        jnp.bfloat16
    )
    key_rot = rotate(key_part.astype(jnp.float32), positions[:, :, None, None]).astype(jnp.bfloat16)
    result = attend(query_rot, key_rot, value_part, cache, lengths)
    return result.reshape(step_count, row_count, per_group * head_size)


def solution(mesh):
    placed = (
        P(None, "fsdp", None),
        P("fsdp", "tp"),
        P("fsdp", None, "tp"),
        P("tp"),
        P(None, "tp"),
        P(),
        P(None, "fsdp", "tp", None, None),
        P("fsdp"),
    )
    return jax.shard_map(
        body, mesh=mesh, in_specs=placed, out_specs=P(None, "fsdp", "tp"), check_vma=False
    )
```

```python
import jax
import jax.numpy as jnp
from jax import lax
from jax.sharding import PartitionSpec as P

HQ = 64
HK = 8
HD = 128

rope_base = 1000000.0
neg_large = -1e30

AXES = ("fsdp", "tp")
N_Z = 4
N_TP = 8


def place_of(index):
    f, t = divmod(index, N_TP)
    z, rest = divmod(f, 4)
    y_lo, core = divmod(rest, 2)
    y_hi, x = divmod(t, 4)
    return z, y_hi * 2 + y_lo, x, core


def index_of(z, y, x, core):
    z, y, x, core = z % 4, y % 4, x % 4, core % 2
    return (z * 4 + (y % 2) * 2 + core) * N_TP + (y // 2) * 4 + x


def moved(value, to):
    pairs = [(i, index_of(*to(*place_of(i)))) for i in range(128)]
    return lax.ppermute(value, AXES, pairs)


def z_by(step):
    return lambda z, y, x, core: (z + step, y, x, core)


def other_core(z, y, x, core):
    return z, y, x, 1 - core


def inner_y(z, y, x, core):
    return z, y ^ 1, x, core


def cross_y_core(z, y, x, core):
    return z, 3 - y, x, 1 - core


def cross_y(z, y, x, core):
    return z, 3 - y, x, core


def far_y(z, y, x, core):
    return z, y + 2, x, core


def rotate(vectors, position):
    head_size = vectors.shape[-1]
    half_size = head_size // 2
    pair_index = jnp.arange(half_size, dtype=jnp.float32)
    inverse = rope_base ** (-2.0 * pair_index / head_size)
    angles = position * inverse
    cos_part = jnp.cos(angles)
    sin_part = jnp.sin(angles)
    first_half = vectors[..., :half_size]
    second = vectors[..., half_size:]
    return jnp.concatenate(
        [first_half * cos_part - second * sin_part, second * cos_part + first_half * sin_part],
        axis=-1,
    )


def attend(queries, key_new, value_new, cache, lengths):
    score_scale = queries.shape[-1] ** (-0.5)
    cached_scores = (
        jnp.einsum("srgqd,rgcd->srgqc", queries, cache[0], preferred_element_type=jnp.float32)
        * score_scale
    )
    fresh_scores = (
        jnp.einsum("srgqd,trgd->srgqt", queries, key_new, preferred_element_type=jnp.float32)
        * score_scale
    )
    slots = jnp.arange(cache.shape[3], dtype=jnp.int32)
    visible_old = (slots[None, :] < lengths[:, None])[None, :, None, None, :]
    step_ids = jnp.arange(queries.shape[0], dtype=jnp.int32)
    visible_new = (step_ids[None, :] <= step_ids[:, None])[:, None, None, None, :]
    cached_scores = jnp.where(visible_old, cached_scores, neg_large)
    fresh_scores = jnp.where(visible_new, fresh_scores, neg_large)
    row_max = jnp.maximum(jnp.max(cached_scores, axis=-1), jnp.max(fresh_scores, axis=-1))[
        ..., None
    ]
    cached_exp = jnp.exp(cached_scores - row_max)
    fresh_exp = jnp.exp(fresh_scores - row_max)
    denominator = jnp.sum(cached_exp, axis=-1, keepdims=True) + jnp.sum(
        fresh_exp, axis=-1, keepdims=True
    )
    cached_weights = (cached_exp / denominator).astype(jnp.bfloat16)
    fresh_weights = (fresh_exp / denominator).astype(jnp.bfloat16)
    result = jnp.einsum(
        "srgqc,rgcd->srgqd", cached_weights, cache[1], preferred_element_type=jnp.float32
    )
    result = result + jnp.einsum(
        "srgqt,trgd->srgqd", fresh_weights, value_new, preferred_element_type=jnp.float32
    )
    return result.astype(jnp.bfloat16)


def near_over_z(block):
    return moved(block, z_by(1)), moved(block, z_by(-1))


def far_over_z(lower, upper):
    half = lower.shape[0] // 2
    return moved(lower[:half], z_by(1)), moved(upper[half:], z_by(-1))


def row_sets(tokens):
    f = lax.axis_index("fsdp")
    z, y_lo, core = f // 4, (f // 2) % 2, f % 2
    flat = tokens.reshape(-1, tokens.shape[-1])
    share = flat.shape[1] // 16

    def slab(dy, dc):
        parts = []
        for dz in (0, -1, 1, 2):
            block = ((z + dz) % 4) * 4 + (y_lo ^ dy) * 2 + (core ^ dc)
            parts.append(lax.dynamic_slice_in_dim(flat, block * share, share, 1))
        return jnp.concatenate(parts, axis=1)

    return {
        (0, 0): slab(0, 0),
        (0, 1): moved(slab(0, 1), other_core),
        (1, 0): moved(slab(1, 0), inner_y),
        (1, 1): moved(slab(1, 1), cross_y_core),
    }


def core_sums(rows, blocks, dy):
    weights = jnp.concatenate(blocks, axis=0)
    theirs = jnp.dot(rows[dy, 1], weights, preferred_element_type=jnp.float32)
    theirs = moved(theirs.astype(jnp.bfloat16), other_core)
    ours = jnp.dot(rows[dy, 0], weights, preferred_element_type=jnp.float32)
    return ours + theirs.astype(jnp.float32)


def body(tokens, w_query, w_keyval, b_query, b_keyval, rotary_perm, cache, lengths):
    step_count, row_count, model_width = tokens.shape
    per_group = HQ // HK
    head_size = rotary_perm.shape[0]

    early = 3 * head_size
    first = jnp.concatenate([w_keyval[:, 0], w_keyval[:, 1], w_query[:, :early]], axis=1)
    second = w_query[:, early:]
    first_bias = jnp.concatenate([b_keyval[0], b_keyval[1], b_query[:early]])
    rows = row_sets(tokens)
    depth = first.shape[0]
    pad = jnp.broadcast_to(b_query[None, early:], (16, b_query.shape[0] - early))
    shifted = moved(jnp.concatenate([second, pad], axis=0), far_y)
    first_near = near_over_z(first)
    shifted, first_near = lax.optimization_barrier((shifted, first_near))
    second, second_bias = shifted[:depth], shifted[depth]
    below, above = first_near
    up = moved(jnp.concatenate([below[: depth // 2], second], axis=0), z_by(1))
    down = moved(jnp.concatenate([above[depth // 2 :], second], axis=0), z_by(-1))
    up, down = lax.optimization_barrier((up, down))
    first_blocks = [first, below, above, up[: depth // 2], down[: depth // 2]]
    below, above = up[depth // 2 :], down[depth // 2 :]
    second_blocks = [second, below, above, *far_over_z(below, above)]

    other = moved(core_sums(rows, first_blocks, 1).astype(jnp.bfloat16), cross_y)
    same = core_sums(rows, first_blocks, 0) + first_bias.astype(jnp.float32)
    same = moved(same.astype(jnp.bfloat16), far_y)
    first_sums = same.astype(jnp.float32) + other.astype(jnp.float32)
    other = moved(core_sums(rows, second_blocks, 1).astype(jnp.bfloat16), inner_y)
    same = core_sums(rows, second_blocks, 0) + second_bias.astype(jnp.float32)
    second_sums = same + other.astype(jnp.float32)

    queries = jnp.concatenate([first_sums[:, 2 * head_size :], second_sums], axis=1)
    queries = queries.reshape(step_count, row_count, 1, per_group, head_size)
    queries = jnp.take(queries, rotary_perm, axis=4)
    key_part = first_sums[:, :head_size].reshape(step_count, row_count, 1, head_size)
    key_part = jnp.take(key_part, rotary_perm, axis=3)
    value_part = first_sums[:, head_size : 2 * head_size]
    value_part = value_part.reshape(step_count, row_count, 1, head_size).astype(jnp.bfloat16)
    positions = (lengths[None, :] + jnp.arange(step_count, dtype=jnp.int32)[:, None]).astype(
        jnp.float32
    )
    query_rot = rotate(queries, positions[:, :, None, None, None]).astype(
        jnp.bfloat16
    )
    key_rot = rotate(key_part, positions[:, :, None, None]).astype(jnp.bfloat16)
    result = attend(query_rot, key_rot, value_part, cache, lengths)
    return result.reshape(step_count, row_count, per_group * head_size)


def solution(mesh):
    placed = (
        P(None, "fsdp", None),
        P("fsdp", "tp"),
        P("fsdp", None, "tp"),
        P("tp"),
        P(None, "tp"),
        P(),
        P(None, "fsdp", "tp", None, None),
        P("fsdp"),
    )
    return jax.shard_map(
        body, mesh=mesh, in_specs=placed, out_specs=P(None, "fsdp", "tp"), check_vma=False
    )
```

```python
import functools

import jax
import jax.numpy as jnp
from jax import lax
from jax.experimental import pallas as pl
from jax.experimental.pallas import tpu as pltpu
from jax.sharding import PartitionSpec as P

rope_base = 1000000.0
neg_large = -1e30
EARLY = 6
TILE = 256
ALL_Z = (0, -1, 1, 2)
BLOCK = 48

AXES = ("fsdp", "tp")
N_Z = 4
N_TP = 8


def place_of(index):
    f, t = divmod(index, N_TP)
    z, rest = divmod(f, 4)
    y_lo, core = divmod(rest, 2)
    y_hi, x = divmod(t, 4)
    return z, y_hi * 2 + y_lo, x, core


def index_of(z, y, x, core):
    z, y, x, core = z % 4, y % 4, x % 4, core % 2
    return (z * 4 + (y % 2) * 2 + core) * N_TP + (y // 2) * 4 + x


def moved(value, to):
    pairs = [(i, index_of(*to(*place_of(i)))) for i in range(128)]
    return lax.ppermute(value, AXES, pairs)


def z_by(step):
    return lambda z, y, x, core: (z + step, y, x, core)


def other_core(z, y, x, core):
    return z, y, x, 1 - core


def inner_y(z, y, x, core):
    return z, y ^ 1, x, core


def inner_y_core(z, y, x, core):
    return z, y ^ 1, x, 1 - core


def cross_y_core(z, y, x, core):
    return z, 3 - y, x, 1 - core


def cross_y(z, y, x, core):
    return z, 3 - y, x, core


def far_y(z, y, x, core):
    return z, y + 2, x, core


def turned(values, turn, cos_part, sin_part):
    high = values.astype(jnp.bfloat16)
    low = (values - high.astype(jnp.float32)).astype(jnp.bfloat16)
    both = jnp.dot(
        jnp.concatenate([high, low], axis=1), turn, preferred_element_type=jnp.float32
    )
    head_size = values.shape[1]
    rotated = both[:, :head_size] * cos_part + both[:, head_size:] * sin_part
    return rotated.astype(jnp.bfloat16).astype(jnp.float32)


def attention_kernel(
    same1,
    other1,
    same2,
    other2,
    last2,
    waves,
    turn,
    lengths,
    cache,
    out,
    held,
    held_q,
    held_s,
    held_o,
    done,
):
    n_parts = cache.shape[1] // BLOCK
    copies = [
        pltpu.make_async_copy(
            cache.at[k, pl.ds(i * BLOCK, BLOCK)],
            held.at[k, pl.ds(i * BLOCK, BLOCK)],
            done.at[k, i],
        )
        for i in range(cache.shape[1] // BLOCK)
        for k in range(2)
    ]
    for copy in copies:
        copy.start()
    for part in range(n_parts):
        attend_block(
            part * BLOCK,
            copies[part * len(copies) // n_parts : (part + 1) * len(copies) // n_parts],
            *(ref.at[:, pl.ds(part * BLOCK, BLOCK)] for ref in (same1, other1, same2, other2, last2, waves)),
            turn,
            lengths.at[pl.ds(part * BLOCK, BLOCK)],
            held,
            out.at[:, pl.ds(part * BLOCK, BLOCK)],
            held_q,
            held_s,
            held_o,
        )


def attend_block(
    first_row,
    copies,
    same1,
    other1,
    same2,
    other2,
    last2,
    waves,
    turn,
    lengths,
    cache,
    out,
    held_q,
    held_s,
    held_o,
):
    steps, rows, head_size = 2, same1.shape[1], turn.shape[1] // 2
    slots = cache.shape[3]
    per_group = out.shape[2] // head_size
    group = steps * per_group
    early = same1.shape[2] // head_size
    table = waves[...].reshape(steps * rows, 2 * head_size)
    cos_part, sin_part = table[:, :head_size], table[:, head_size:]

    def head(parts, index):
        columns = pl.ds(index * head_size, head_size)
        total = sum(part[:, :, columns].astype(jnp.float32) for part in parts)
        return total.reshape(steps * rows, head_size)

    parts1, parts2 = (same1, other1), (same2, other2, last2)
    keys = turned(head(parts2, 0), turn[...], cos_part, sin_part)
    values = head(parts2, 1).astype(jnp.bfloat16).astype(jnp.float32)
    for h in range(per_group):
        raw = head(parts1, h) if h < early else head(parts2, h - early + 2)
        query = turned(raw, turn[...], cos_part, sin_part)
        for s in range(steps):
            held_q[pl.ds(s * per_group + h, rows, stride=group), :] = query[
                s * rows : (s + 1) * rows
            ]

    queries = held_q[...]
    narrow = queries.astype(jnp.bfloat16)
    scale = head_size ** (-0.5)
    for copy in copies[::2]:
        copy.wait()
    for r in range(rows):
        held_s[r * group : (r + 1) * group, :] = lax.dot_general(
            narrow[r * group : (r + 1) * group],
            cache[0, first_row + r, 0],
            (((1,), (1,)), ((), ())),
            preferred_element_type=jnp.float32,
        )
    old = held_s[...].reshape(rows, group, slots) * scale
    visible = lax.broadcasted_iota(jnp.int32, (rows, slots), 1) < lengths[...]
    old = jnp.where(visible[:, None, :], old, neg_large)
    cube = queries.reshape(rows, group, head_size)
    new0 = jnp.sum(cube * keys[:rows][:, None, :], axis=2, keepdims=True) * scale
    new1 = jnp.sum(cube * keys[rows:][:, None, :], axis=2, keepdims=True) * scale
    later = lax.broadcasted_iota(jnp.int32, (rows, group, 1), 1) >= per_group
    new1 = jnp.where(later, new1, neg_large)
    top = jnp.maximum(jnp.max(old, axis=2, keepdims=True), jnp.maximum(new0, new1))
    old, new0, new1 = jnp.exp(old - top), jnp.exp(new0 - top), jnp.exp(new1 - top)
    share = 1.0 / (jnp.sum(old, axis=2, keepdims=True) + new0 + new1)
    weights = (old * share).astype(jnp.bfloat16).reshape(rows * group, slots)
    new0 = (new0 * share).astype(jnp.bfloat16).astype(jnp.float32)
    new1 = (new1 * share).astype(jnp.bfloat16).astype(jnp.float32)
    fresh = new0 * values[:rows][:, None, :] + new1 * values[rows:][:, None, :]
    for copy in copies[1::2]:
        copy.wait()
    for r in range(rows):
        total = fresh[r] + jnp.dot(
            weights[r * group : (r + 1) * group],
            cache[1, first_row + r, 0],
            preferred_element_type=jnp.float32,
        )
        held_o[pl.ds(r, group, stride=rows), :] = total
    for s in range(steps):
        for h in range(per_group):
            part = held_o[pl.ds((s * per_group + h) * rows, rows), :]
            out[s, :, h * head_size : (h + 1) * head_size] = part.astype(out.dtype)


def attention(same1, other1, same2, other2, last2, waves, turn, lengths, cache):
    steps, rows, slots, head_size = 2, cache.shape[1], cache.shape[3], cache.shape[4]
    width = same1.shape[1] + same2.shape[1] - 2 * head_size
    group = steps * width // head_size
    split = lambda a: a.reshape(steps, rows, a.shape[-1])
    here = pl.BlockSpec(memory_space=pltpu.VMEM)
    return pl.pallas_call(
        attention_kernel,
        out_shape=jax.ShapeDtypeStruct((steps, rows, width), jnp.bfloat16),
        in_specs=[here] * 8 + [pl.BlockSpec(memory_space=pl.ANY)],
        out_specs=here,
        scratch_shapes=[
            pltpu.VMEM(cache.shape, cache.dtype),
            pltpu.VMEM((BLOCK * group, head_size), jnp.float32),
            pltpu.VMEM((BLOCK * group, slots), jnp.float32),
            pltpu.VMEM((BLOCK * group, head_size), jnp.float32),
            pltpu.SemaphoreType.DMA((2, rows // BLOCK)),
        ],
        compiler_params=pltpu.CompilerParams(vmem_limit_bytes=28 * 2**20),
        cost_estimate=pl.CostEstimate(
            flops=4 * rows * group * slots * head_size,
            bytes_accessed=2 * cache.size,
            transcendentals=rows * group * slots,
        ),
    )(
        *(split(a) for a in (same1, other1, same2, other2, last2, waves)),
        turn,
        lengths,
        pltpu.with_memory_space_constraint(cache, pltpu.HBM),
    )


def turning(rotary_perm):
    head_size = rotary_perm.shape[0]
    chosen = jnp.arange(head_size, dtype=jnp.int32)[:, None] == rotary_perm[None, :]
    chosen = chosen.astype(jnp.bfloat16)
    half = head_size // 2
    partner = jnp.concatenate([-chosen[:, half:], chosen[:, :half]], axis=1)
    once = jnp.concatenate([chosen, partner], axis=1)
    return jnp.concatenate([once, once], axis=0)


def wave_table(lengths, steps, head_size):
    pair_index = jnp.arange(head_size // 2, dtype=jnp.float32)
    inverse = rope_base ** (-2.0 * pair_index / head_size)
    places = lengths[None, :] + jnp.arange(steps, dtype=jnp.int32)[:, None]
    angles = places.astype(jnp.float32)[:, :, None] * inverse
    cos_part, sin_part = jnp.cos(angles), jnp.sin(angles)
    table = jnp.concatenate([cos_part, cos_part, sin_part, sin_part], axis=2)
    return table.reshape(-1, 2 * head_size)


def near_over_z(block):
    return moved(block, z_by(1)), moved(block, z_by(-1))


def slabs(tokens):
    f = lax.axis_index("fsdp")
    z, y_lo, core = f // 4, (f // 2) % 2, f % 2
    flat = tokens.reshape(-1, tokens.shape[-1])
    share = flat.shape[1] // 16

    def slab(dy, dc, steps):
        parts = []
        for dz in steps:
            block = ((z + dz) % 4) * 4 + (y_lo ^ dy) * 2 + (core ^ dc)
            parts.append(lax.dynamic_slice_in_dim(flat, block * share, share, 1))
        return jnp.concatenate(parts, axis=1)

    return slab


def product_kernel(n_rows, n_weights, tiles, *refs):
    row_refs, weight_refs = refs[:n_rows], refs[n_rows : n_rows + n_weights]
    out = refs[-1]
    for tile, spans in enumerate(tiles):
        columns = pl.ds(tile * TILE, TILE)
        total, at, which = None, 0, 0
        for source, row, column, depth in spans:
            if at == row_refs[which].shape[1]:
                at, which = 0, which + 1
            part = jnp.dot(
                row_refs[which][:, at : at + depth],
                weight_refs[source][row : row + depth, column : column + TILE],
                preferred_element_type=jnp.float32,
            )
            total = part if total is None else total + part
            at += depth
        for extra in refs[n_rows + n_weights : -1]:
            total = total + extra[:, columns].astype(jnp.float32)
        out[:, columns] = total.astype(out.dtype)


def product(rows, weights, tiles, dtype, *extras):
    operands = [*rows, *weights, *extras]
    here = pl.BlockSpec(memory_space=pltpu.VMEM)
    return pl.pallas_call(
        functools.partial(product_kernel, len(rows), len(weights), tiles),
        out_shape=pltpu.VMEM((rows[0].shape[0], len(tiles) * TILE), dtype),
        in_specs=[here] * len(operands),
        out_specs=here,
        compiler_params=pltpu.CompilerParams(vmem_limit_bytes=4 * 2**20),
        cost_estimate=pl.CostEstimate(flops=1, bytes_accessed=1, transcendentals=0),
    )(*(pltpu.with_memory_space_constraint(a, pltpu.VMEM) for a in operands))


def packed(half, whole):
    width, rest = whole.shape[1], half.shape[1] - whole.shape[1]
    depth = half.shape[0] * rest // width
    pieces = [half[i * depth : (i + 1) * depth, width:] for i in range(width // rest)]
    return jnp.concatenate([whole, half[:, :width], jnp.concatenate(pieces, axis=1)], axis=0)


def body(tokens, w_query, w_keyval, b_query, b_keyval, rotary_perm, cache, lengths):
    head_size = rotary_perm.shape[0]
    tables = (
        wave_table(lengths, tokens.shape[0], head_size),
        turning(rotary_perm),
        lengths.reshape(-1, 1),
    )
    early = EARLY * head_size
    depth = w_query.shape[0]
    half = depth // 2
    first, first_bias = w_query[:, :early], b_query[None, :early]
    second = jnp.concatenate([w_keyval[:, 0], w_keyval[:, 1], w_query[:, early:]], axis=1)
    second_bias = jnp.concatenate([b_keyval[0], b_keyval[1], b_query[early:]])
    second_bias = jnp.broadcast_to(second_bias[None], (16, second_bias.shape[0]))
    slab = slabs(tokens)

    below, above = moved(first, z_by(1)), moved(first, z_by(-1))
    shifted = moved(jnp.concatenate([second, second_bias], axis=0), far_y)
    shifted, below, above, out01, out10, out11 = lax.optimization_barrier(
        (shifted, below, above, slab(0, 1, ALL_Z), slab(1, 0, ALL_Z), slab(1, 1, ALL_Z))
    )
    up = moved(packed(below[:half], shifted[:depth]), z_by(1))
    down = moved(packed(above[half:], shifted[:depth]), z_by(-1))
    rows01 = moved(out01, other_core)
    rows10 = moved(out10, inner_y)
    rows11 = moved(out11, cross_y_core)
    up, down, rows00, tables = lax.optimization_barrier(
        (up, down, slab(0, 0, ALL_Z), tables)
    )
    far_up = moved(up[:half], z_by(1))
    far_down = moved(down[half:depth], z_by(-1))

    width, rest = second.shape[1], early - second.shape[1]
    tiles = []
    for column in range(0, early, TILE):
        spans = [(i, 0, column, depth) for i in range(3)]
        for i in (3, 4):
            if column < width:
                spans.append((i, depth, column, half))
            else:
                count = width // rest
                for j in range(count):
                    spans.append((i, depth + half, column - width + j * rest, half // count))
        tiles.append(tuple(spans))
    weights = first, below, above, up, down
    theirs0 = product([rows01], weights, tiles, jnp.bfloat16)
    theirs0, rows10, rows11 = lax.optimization_barrier((theirs0, rows10, rows11))
    theirs0 = moved(theirs0, other_core)
    theirs1 = moved(product([rows11], weights, tiles, jnp.bfloat16), other_core)
    same = product([rows00], weights, tiles, jnp.bfloat16, theirs0, first_bias)
    other = product([rows10], weights, tiles, jnp.bfloat16, theirs1)
    first_parts = moved(same, far_y), moved(other, cross_y)
    far_up, far_down, _, _ = lax.optimization_barrier((far_up, far_down, same, other))

    tiles = []
    for column in range(0, width, TILE):
        spans = [(i, 0, column, depth) for i in range(3)]
        tiles.append((*spans, (3, 0, column, half), (4, 0, column, half)))
    weights = shifted, up, down, far_up, far_down
    inner = moved(product([rows10], weights, tiles, jnp.bfloat16), inner_y)
    crossed = moved(product([rows11], weights, tiles, jnp.bfloat16), inner_y_core)
    theirs = moved(product([rows01], weights, tiles, jnp.bfloat16), other_core)
    own = product([rows00], weights, tiles, jnp.float32, theirs, shifted[depth : depth + 1])
    return attention(*first_parts, own, inner, crossed, *tables, cache)


def solution(mesh):
    placed = (
        P(None, "fsdp", None),
        P("fsdp", "tp"),
        P("fsdp", None, "tp"),
        P("tp"),
        P(None, "tp"),
        P(),
        P(None, "fsdp", "tp", None, None),
        P("fsdp"),
    )
    return jax.shard_map(
        body, mesh=mesh, in_specs=placed, out_specs=P(None, "fsdp", "tp"), check_vma=False
    )
```

```python
import functools

import jax
import jax.numpy as jnp
from jax import lax
from jax.experimental import pallas as pl
from jax.experimental.pallas import tpu as pltpu
from jax.sharding import PartitionSpec as P

rope_base = 1000000.0
neg_large = -1e30
EARLY = 6
TILE = 256
ALL_Z = (0, -1, 1, 2)
BLOCK = 48

AXES = ("fsdp", "tp")
N_Z = 4
N_TP = 8


def place_of(index):
    f, t = divmod(index, N_TP)
    z, rest = divmod(f, 4)
    y_lo, core = divmod(rest, 2)
    y_hi, x = divmod(t, 4)
    return z, y_hi * 2 + y_lo, x, core


def index_of(z, y, x, core):
    z, y, x, core = z % 4, y % 4, x % 4, core % 2
    return (z * 4 + (y % 2) * 2 + core) * N_TP + (y // 2) * 4 + x


def moved(value, to):
    pairs = [(i, index_of(*to(*place_of(i)))) for i in range(128)]
    return lax.ppermute(value, AXES, pairs)


def z_by(step):
    return lambda z, y, x, core: (z + step, y, x, core)


def other_core(z, y, x, core):
    return z, y, x, 1 - core


def inner_y(z, y, x, core):
    return z, y ^ 1, x, core


def inner_y_core(z, y, x, core):
    return z, y ^ 1, x, 1 - core


def cross_y_core(z, y, x, core):
    return z, 3 - y, x, 1 - core


def cross_y(z, y, x, core):
    return z, 3 - y, x, core


def far_y(z, y, x, core):
    return z, y + 2, x, core


def turned(values, turn, cos_part, sin_part):
    high = values.astype(jnp.bfloat16)
    low = (values - high.astype(jnp.float32)).astype(jnp.bfloat16)
    both = jnp.dot(
        jnp.concatenate([high, low], axis=1), turn, preferred_element_type=jnp.float32
    )
    head_size = values.shape[1]
    rotated = both[:, :head_size] * cos_part + both[:, head_size:] * sin_part
    return rotated.astype(jnp.bfloat16).astype(jnp.float32)


def attention_kernel(
    same1,
    other1,
    same2,
    other2,
    last2,
    waves,
    turn,
    lengths,
    cache,
    out,
    held,
    held_q,
    held_s,
    held_o,
    done,
):
    n_parts = cache.shape[1] // BLOCK
    copies = [
        pltpu.make_async_copy(
            cache.at[k, pl.ds(i * BLOCK, BLOCK)],
            held.at[k, pl.ds(i * BLOCK, BLOCK)],
            done.at[k, i],
        )
        for i in range(cache.shape[1] // BLOCK)
        for k in range(2)
    ]
    for copy in copies:
        copy.start()
    for part in range(n_parts):
        attend_block(
            part * BLOCK,
            copies[part * len(copies) // n_parts : (part + 1) * len(copies) // n_parts],
            *(ref.at[:, pl.ds(part * BLOCK, BLOCK)] for ref in (same1, other1, same2, other2, last2, waves)),
            turn,
            lengths.at[pl.ds(part * BLOCK, BLOCK)],
            held,
            out.at[:, pl.ds(part * BLOCK, BLOCK)],
            held_q,
            held_s,
            held_o,
        )


def attend_block(
    first_row,
    copies,
    same1,
    other1,
    same2,
    other2,
    last2,
    waves,
    turn,
    lengths,
    cache,
    out,
    held_q,
    held_s,
    held_o,
):
    steps, rows, head_size = 2, same1.shape[1], turn.shape[1] // 2
    slots = cache.shape[3]
    per_group = out.shape[2] // head_size
    group = steps * per_group
    early = same1.shape[2] // head_size
    table = waves[...].reshape(steps * rows, 2 * head_size)
    cos_part, sin_part = table[:, :head_size], table[:, head_size:]

    def head(parts, index):
        columns = pl.ds(index * head_size, head_size)
        total = sum(part[:, :, columns].astype(jnp.float32) for part in parts)
        return total.reshape(steps * rows, head_size)

    parts1, parts2 = (same1, other1), (same2, other2, last2)
    keys = turned(head(parts2, 0), turn[...], cos_part, sin_part)
    values = head(parts2, 1).astype(jnp.bfloat16).astype(jnp.float32)
    for h in range(per_group):
        raw = head(parts1, h) if h < early else head(parts2, h - early + 2)
        query = turned(raw, turn[...], cos_part, sin_part)
        for s in range(steps):
            held_q[pl.ds(s * per_group + h, rows, stride=group), :] = query[
                s * rows : (s + 1) * rows
            ]

    queries = held_q[...]
    narrow = queries.astype(jnp.bfloat16)
    scale = head_size ** (-0.5)
    for copy in copies[::2]:
        copy.wait()
    for r in range(rows):
        held_s[r * group : (r + 1) * group, :] = lax.dot_general(
            narrow[r * group : (r + 1) * group],
            cache[0, first_row + r, 0],
            (((1,), (1,)), ((), ())),
            preferred_element_type=jnp.float32,
        )
    old = held_s[...].reshape(rows, group, slots) * scale
    visible = lax.broadcasted_iota(jnp.int32, (rows, slots), 1) < lengths[...]
    old = jnp.where(visible[:, None, :], old, neg_large)
    cube = queries.reshape(rows, group, head_size)
    new0 = jnp.sum(cube * keys[:rows][:, None, :], axis=2, keepdims=True) * scale
    new1 = jnp.sum(cube * keys[rows:][:, None, :], axis=2, keepdims=True) * scale
    later = lax.broadcasted_iota(jnp.int32, (rows, group, 1), 1) >= per_group
    new1 = jnp.where(later, new1, neg_large)
    top = jnp.maximum(jnp.max(old, axis=2, keepdims=True), jnp.maximum(new0, new1))
    old, new0, new1 = jnp.exp(old - top), jnp.exp(new0 - top), jnp.exp(new1 - top)
    share = 1.0 / (jnp.sum(old, axis=2, keepdims=True) + new0 + new1)
    weights = (old * share).astype(jnp.bfloat16).reshape(rows * group, slots)
    new0 = (new0 * share).astype(jnp.bfloat16).astype(jnp.float32)
    new1 = (new1 * share).astype(jnp.bfloat16).astype(jnp.float32)
    fresh = new0 * values[:rows][:, None, :] + new1 * values[rows:][:, None, :]
    for copy in copies[1::2]:
        copy.wait()
    for r in range(rows):
        total = fresh[r] + jnp.dot(
            weights[r * group : (r + 1) * group],
            cache[1, first_row + r, 0],
            preferred_element_type=jnp.float32,
        )
        held_o[pl.ds(r, group, stride=rows), :] = total
    for s in range(steps):
        for h in range(per_group):
            part = held_o[pl.ds((s * per_group + h) * rows, rows), :]
            out[s, :, h * head_size : (h + 1) * head_size] = part.astype(out.dtype)


def attention(same1, other1, same2, other2, last2, waves, turn, lengths, cache):
    steps, rows, slots, head_size = 2, cache.shape[1], cache.shape[3], cache.shape[4]
    width = same1.shape[1] + same2.shape[1] - 2 * head_size
    group = steps * width // head_size
    split = lambda a: a.reshape(steps, rows, a.shape[-1])
    here = pl.BlockSpec(memory_space=pltpu.VMEM)
    return pl.pallas_call(
        attention_kernel,
        out_shape=jax.ShapeDtypeStruct((steps, rows, width), jnp.bfloat16),
        in_specs=[here] * 8 + [pl.BlockSpec(memory_space=pl.ANY)],
        out_specs=here,
        scratch_shapes=[
            pltpu.VMEM(cache.shape, cache.dtype),
            pltpu.VMEM((BLOCK * group, head_size), jnp.float32),
            pltpu.VMEM((BLOCK * group, slots), jnp.float32),
            pltpu.VMEM((BLOCK * group, head_size), jnp.float32),
            pltpu.SemaphoreType.DMA((2, rows // BLOCK)),
        ],
        compiler_params=pltpu.CompilerParams(vmem_limit_bytes=28 * 2**20),
        cost_estimate=pl.CostEstimate(
            flops=4 * rows * group * slots * head_size,
            bytes_accessed=2 * cache.size,
            transcendentals=rows * group * slots,
        ),
    )(
        *(split(a) for a in (same1, other1, same2, other2, last2, waves)),
        turn,
        lengths,
        pltpu.with_memory_space_constraint(cache, pltpu.HBM),
    )


def turning(rotary_perm):
    head_size = rotary_perm.shape[0]
    chosen = jnp.arange(head_size, dtype=jnp.int32)[:, None] == rotary_perm[None, :]
    chosen = chosen.astype(jnp.bfloat16)
    half = head_size // 2
    partner = jnp.concatenate([-chosen[:, half:], chosen[:, :half]], axis=1)
    once = jnp.concatenate([chosen, partner], axis=1)
    return jnp.concatenate([once, once], axis=0)


def wave_table(lengths, steps, head_size):
    pair_index = jnp.arange(head_size // 2, dtype=jnp.float32)
    inverse = rope_base ** (-2.0 * pair_index / head_size)
    places = lengths[None, :] + jnp.arange(steps, dtype=jnp.int32)[:, None]
    angles = places.astype(jnp.float32)[:, :, None] * inverse
    cos_part, sin_part = jnp.cos(angles), jnp.sin(angles)
    table = jnp.concatenate([cos_part, cos_part, sin_part, sin_part], axis=2)
    return table.reshape(-1, 2 * head_size)


def near_over_z(block):
    return moved(block, z_by(1)), moved(block, z_by(-1))


def slabs(tokens):
    f = lax.axis_index("fsdp")
    z, y_lo, core = f // 4, (f // 2) % 2, f % 2
    flat = tokens.reshape(-1, tokens.shape[-1])
    share = flat.shape[1] // 16

    def slab(dy, dc, steps):
        parts = []
        for dz in steps:
            block = ((z + dz) % 4) * 4 + (y_lo ^ dy) * 2 + (core ^ dc)
            parts.append(lax.dynamic_slice_in_dim(flat, block * share, share, 1))
        return jnp.concatenate(parts, axis=1)

    return slab


def product_kernel(n_rows, n_weights, tiles, *refs):
    row_refs, weight_refs = refs[:n_rows], refs[n_rows : n_rows + n_weights]
    out = refs[-1]
    for tile, spans in enumerate(tiles):
        columns = pl.ds(tile * TILE, TILE)
        total, at, which = None, 0, 0
        for source, row, column, depth in spans:
            if at == row_refs[which].shape[1]:
                at, which = 0, which + 1
            part = jnp.dot(
                row_refs[which][:, at : at + depth],
                weight_refs[source][row : row + depth, column : column + TILE],
                preferred_element_type=jnp.float32,
            )
            total = part if total is None else total + part
            at += depth
        for extra in refs[n_rows + n_weights : -1]:
            total = total + extra[:, columns].astype(jnp.float32)
        out[:, columns] = total.astype(out.dtype)


def product(rows, weights, tiles, dtype, *extras):
    operands = [*rows, *weights, *extras]
    here = pl.BlockSpec(memory_space=pltpu.VMEM)
    return pl.pallas_call(
        functools.partial(product_kernel, len(rows), len(weights), tiles),
        out_shape=pltpu.VMEM((rows[0].shape[0], len(tiles) * TILE), dtype),
        in_specs=[here] * len(operands),
        out_specs=here,
        compiler_params=pltpu.CompilerParams(vmem_limit_bytes=4 * 2**20),
        cost_estimate=pl.CostEstimate(flops=1, bytes_accessed=1, transcendentals=0),
    )(*(pltpu.with_memory_space_constraint(a, pltpu.VMEM) for a in operands))


def packed(half, whole):
    width, rest = whole.shape[1], half.shape[1] - whole.shape[1]
    depth = half.shape[0] * rest // width
    pieces = [half[i * depth : (i + 1) * depth, width:] for i in range(width // rest)]
    return jnp.concatenate([whole, half[:, :width], jnp.concatenate(pieces, axis=1)], axis=0)


def body(tokens, w_query, w_keyval, b_query, b_keyval, rotary_perm, cache, lengths):
    head_size = rotary_perm.shape[0]
    tables = (
        wave_table(lengths, tokens.shape[0], head_size),
        turning(rotary_perm),
        lengths.reshape(-1, 1),
    )
    early = EARLY * head_size
    depth = w_query.shape[0]
    half = depth // 2
    first, first_bias = w_query[:, :early], b_query[None, :early]
    second = jnp.concatenate([w_keyval[:, 0], w_keyval[:, 1], w_query[:, early:]], axis=1)
    second_bias = jnp.concatenate([b_keyval[0], b_keyval[1], b_query[early:]])
    second_bias = jnp.broadcast_to(second_bias[None], (16, second_bias.shape[0]))

    second = jnp.concatenate([second, second_bias], axis=0)
    second, tokens = lax.optimization_barrier((second, tokens))
    slab = slabs(tokens)
    below, above = moved(first, z_by(1)), moved(first, z_by(-1))
    shifted = moved(second, far_y)
    rows10 = moved(slab(1, 0, ALL_Z), inner_y)
    rows11 = moved(slab(1, 1, ALL_Z), cross_y_core)
    shifted, below, above, out01 = lax.optimization_barrier(
        (shifted, below, above, slab(0, 1, ALL_Z))
    )
    up = moved(packed(below[:half], shifted[:depth]), z_by(1))
    down = moved(packed(above[half:], shifted[:depth]), z_by(-1))
    rows01 = moved(out01, other_core)
    up, down, rows00, tables = lax.optimization_barrier(
        (up, down, slab(0, 0, ALL_Z), tables)
    )
    far_up = moved(up[:half], z_by(1))
    far_down = moved(down[half:depth], z_by(-1))

    width, rest = shifted.shape[1], early - shifted.shape[1]
    tiles = []
    for column in range(0, early, TILE):
        spans = [(i, 0, column, depth) for i in range(3)]
        for i in (3, 4):
            if column < width:
                spans.append((i, depth, column, half))
            else:
                count = width // rest
                for j in range(count):
                    spans.append((i, depth + half, column - width + j * rest, half // count))
        tiles.append(tuple(spans))
    weights = first, below, above, up, down
    theirs0 = product([rows01], weights, tiles, jnp.bfloat16)
    theirs0, rows10, rows11 = lax.optimization_barrier((theirs0, rows10, rows11))
    theirs0 = moved(theirs0, other_core)
    theirs1 = moved(product([rows11], weights, tiles, jnp.bfloat16), other_core)
    same = product([rows00], weights, tiles, jnp.bfloat16, theirs0, first_bias)
    other = product([rows10], weights, tiles, jnp.bfloat16, theirs1)
    first_parts = moved(same, far_y), moved(other, cross_y)

    tiles = []
    for column in range(0, width, TILE):
        spans = [(i, 0, column, depth) for i in range(3)]
        tiles.append((*spans, (3, 0, column, half), (4, 0, column, half)))
    weights = shifted, up, down, far_up, far_down
    inner = moved(product([rows10], weights, tiles, jnp.bfloat16), inner_y)
    crossed = moved(product([rows11], weights, tiles, jnp.bfloat16), inner_y_core)
    theirs = moved(product([rows01], weights, tiles, jnp.bfloat16), other_core)
    own = product([rows00], weights, tiles, jnp.float32, theirs, shifted[depth : depth + 1])
    return attention(*first_parts, own, inner, crossed, *tables, cache)


def solution(mesh):
    placed = (
        P(None, "fsdp", None),
        P("fsdp", "tp"),
        P("fsdp", None, "tp"),
        P("tp"),
        P(None, "tp"),
        P(),
        P(None, "fsdp", "tp", None, None),
        P("fsdp"),
    )
    return jax.shard_map(
        body, mesh=mesh, in_specs=placed, out_specs=P(None, "fsdp", "tp"), check_vma=False
    )
```
